256 devices in a mesh: vid: 64 (over z_hi, x, y), tp: 4 (over z_lo, core).
Axes of the slice: x: 4, y: 4, z: 8 (z_hi: 4, z_lo: 2; z = z_hi * 2 + z_lo), core: 2. Of those that a mesh axis runs over, the one named last changes fastest.
Arguments:
- video_x: bfloat16 [32768, 3072], P('vid', 'tp'), may hold values from -6 to 6
- audio_x: bfloat16 [4096, 3072], P('vid', 'tp'), may hold values from -6 to 6
- video_kv: bfloat16 [32768, 2, 1536], P('vid', None, 'tp'), may hold values from -500 to 500
- audio_kv: bfloat16 [4096, 2, 1536], P('vid', None, 'tp'), may hold values from -500 to 500
- wq_video: bfloat16 [3072, 1536], P(None, 'tp'), may hold values from -0.109375 to 0.109375
- wo_video: bfloat16 [1536, 3072], P('tp'), may hold values from -0.15625 to 0.15625
- wq_audio: bfloat16 [3072, 1536], P(None, 'tp'), may hold values from -0.109375 to 0.109375
- wo_audio: bfloat16 [1536, 3072], P('tp'), may hold values from -0.15625 to 0.15625
- block_list: int32 [256, 3], replicated, may hold values from 0 to 31, as said below
- video_len: int32 [1], replicated, may hold values from 31872 to 32768
- audio_len: int32 [1], replicated, may hold values from 3969 to 4096
Outputs:
- video_out: bfloat16 [32768, 3072], P('vid', 'tp')
- audio_out: bfloat16 [4096, 3072], P('vid', 'tp')
The draws below stay inside these ranges and needn't reach their ends.
Inputs may be any that keep to these rules, and one draw needn't show every extreme that they name: `block_list`: row v holds three audio blocks, each within 2 of floor(v / 8), and floor(v / 8) itself is among them; an entry may repeat.
All inputs are finite; a program needn't handle non-finite values.
Results may differ from the reference program's by a relative error of at most 0.015.
The reference program's roundings to bfloat16 on the way (of `q_video`, `q_audio`, `attn_video` and `attn_audio`) count: a program that leaves them out, or rounds other values in their place, can miss the bound.
Values may be sent and summed in bfloat16 or wider, within the bound.
A program may use at most 128 MiB of HBM per device.

```python
import jax
import jax.numpy as jnp
from jax import lax

D = 3072
HEADS = 12
HDIM = 128
BLOCK = 128
RATIO = 8
HD = 1536
VID_DEV = 512
VIDEO = 32768
AUDIO = 4096
VBLK = 256


def draw_video_kv(key, part):
    key = jax.random.fold_in(key, 3)
    base_key = jax.random.fold_in(key, 0)
    parts = jnp.clip(jax.random.normal(base_key, (VIDEO, 2, HD), jnp.float32), -5.0, 5.0)
    boost = jnp.ones((VIDEO, 1, 1), jnp.float32)
    scale = jnp.array([2.0, 3.0], jnp.float32).reshape(1, 2, 1)
    key_part = jnp.array([1.0, 0.0], jnp.float32).reshape(1, 2, 1)
    return (parts * scale * (1.0 + key_part * (boost - 1.0))).astype(jnp.bfloat16)


def draw_audio_kv(key, part):
    key = jax.random.fold_in(key, 5)
    base_key = jax.random.fold_in(key, 0)
    parts = jnp.clip(jax.random.normal(base_key, (AUDIO, 2, HD), jnp.float32), -5.0, 5.0)
    boost = jnp.ones((AUDIO, 1, 1), jnp.float32)
    scale = jnp.array([2.0, 3.0], jnp.float32).reshape(1, 2, 1)
    key_part = jnp.array([1.0, 0.0], jnp.float32).reshape(1, 2, 1)
    return (parts * scale * (1.0 + key_part * (boost - 1.0))).astype(jnp.bfloat16)


def draw_block_list(key, part):
    key = jax.random.fold_in(key, 7)
    centre = jnp.arange(VBLK, dtype=jnp.int32) // RATIO
    offset = jax.random.randint(key, (VBLK, 1), -1, 2, dtype=jnp.int32)
    spread = jnp.arange(3, dtype=jnp.int32)[None, :] - 1
    return jnp.clip(centre[:, None] + offset + spread, 0, VBLK // RATIO - 1).astype(jnp.int32)


def level_of(stream_key, dims, cuts, low, top_value):
    level = 1.0
    for axis_at, shards_of in cuts:
        steps = jax.random.uniform(jax.random.fold_in(jax.random.fold_in(stream_key, 6), axis_at), (shards_of,), jnp.float32, low / len(cuts), top_value / len(cuts))
        level = level * jnp.repeat(jnp.exp(steps), dims[axis_at] // shards_of).reshape((-1,) + (1,) * (len(dims) - 1 - axis_at))
    return level


def bell_draw(stream_key, dims, deviation, limit, cuts=(), kind=jnp.bfloat16):
    loudness = level_of(stream_key, dims, cuts, -0.22, 0.18) if cuts else 1.0
    values = jax.random.normal(stream_key, dims, jnp.float32) * deviation * loudness
    return jnp.minimum(jnp.maximum(values, -limit), limit).astype(kind)


def setup_inputs(seed: int = 0) -> dict:
    keys = jax.random.split(jax.random.key(seed), 12)
    video_x = bell_draw(keys[0], (VIDEO, D), 1.0, 6.0, ((0, 64), (1, 4)))
    audio_x = bell_draw(keys[1], (AUDIO, D), 1.0, 6.0, ((0, 64), (1, 4)))
    video_kv = draw_video_kv(jax.random.fold_in(keys[11], 71), 0)
    audio_kv = draw_audio_kv(jax.random.fold_in(keys[11], 71), 0)
    wq_video = bell_draw(keys[4], (D, HD), D ** -0.5, 0.109375, ((1, 4),))
    wo_video = bell_draw(keys[5], (HD, D), HD ** -0.5, 0.15625, ((0, 4),))
    wq_audio = bell_draw(keys[6], (D, HD), D ** -0.5, 0.109375, ((1, 4),))
    wo_audio = bell_draw(keys[7], (HD, D), HD ** -0.5, 0.15625, ((0, 4),))
    block_list = draw_block_list(jax.random.fold_in(keys[11], 71), 0)
    video_len = jax.random.randint(keys[9], (1,), VIDEO - 7 * BLOCK, VIDEO + 1).astype(jnp.int32)
    audio_len = jax.random.randint(keys[10], (1,), AUDIO - BLOCK + 1, AUDIO + 1).astype(jnp.int32)
    return dict(video_x=video_x, audio_x=audio_x, video_kv=video_kv, audio_kv=audio_kv, wq_video=wq_video, wo_video=wo_video, wq_audio=wq_audio, wo_audio=wo_audio, block_list=block_list, video_len=video_len, audio_len=audio_len)


NEGATIVE = -1.0e30


def attend(queries, key_rows, values, allowed):
    scores = jnp.einsum("qhd,khd->hqk", queries.astype(jnp.float32), key_rows.astype(jnp.float32), precision=lax.Precision.HIGHEST) * (HDIM ** -0.5)
    scores = jnp.where(allowed[None], scores, NEGATIVE)
    row_peak = jnp.max(scores, axis=-1, keepdims=True)
    weights = jnp.where(allowed[None], jnp.exp(scores - row_peak), 0.0)
    weight_sum = jnp.sum(weights, axis=-1)
    weighted = jnp.einsum("hqk,khd->qhd", weights.astype(jnp.bfloat16).astype(jnp.float32), values.astype(jnp.float32), precision=lax.Precision.HIGHEST)
    return (weighted / weight_sum.T[:, :, None]).astype(jnp.bfloat16)


def reference(video_x, audio_x, video_kv, audio_kv, wq_video, wo_video, wq_audio, wo_audio, block_list, video_len, audio_len):
    q_video = jnp.dot(video_x, wq_video, preferred_element_type=jnp.float32).astype(jnp.bfloat16).reshape(VIDEO, HEADS, HDIM)
    q_audio = jnp.dot(audio_x, wq_audio, preferred_element_type=jnp.float32).astype(jnp.bfloat16).reshape(AUDIO, HEADS, HDIM)
    video_lists = jnp.repeat(block_list, BLOCK, axis=0)
    audio_keys = audio_kv[:, 0].reshape(AUDIO, HEADS, HDIM)
    audio_values = audio_kv[:, 1].reshape(AUDIO, HEADS, HDIM)
    video_keys = video_kv[:, 0].reshape(VIDEO, HEADS, HDIM)
    video_values = video_kv[:, 1].reshape(VIDEO, HEADS, HDIM)
    audio_positions = jnp.arange(AUDIO, dtype=jnp.int32)
    audio_blocks = audio_positions // BLOCK
    audio_valid = audio_positions < audio_len[0]
    video_valid = jnp.arange(VIDEO, dtype=jnp.int32) < video_len[0]

    def video_rows(block_number):
        first_row = (block_number * VID_DEV).astype(jnp.int32)
        query_rows = lax.dynamic_slice_in_dim(q_video, first_row, VID_DEV, 0)
        row_lists = lax.dynamic_slice_in_dim(video_lists, first_row, VID_DEV, 0)
        allowed = jnp.any(row_lists[:, None, :] == audio_blocks[None, :, None], axis=-1) & audio_valid[None]
        return attend(query_rows, audio_keys, audio_values, allowed)

    attn_video = lax.map(video_rows, jnp.arange(VIDEO // VID_DEV, dtype=jnp.int32)).reshape(VIDEO, HD)

    def audio_rows(block_number):
        first_row = (block_number * BLOCK).astype(jnp.int32)
        query_rows = lax.dynamic_slice_in_dim(q_audio, first_row, BLOCK, 0)
        linked = jnp.any(video_lists == block_number, axis=-1) & video_valid
        allowed = jnp.broadcast_to(linked[None], (BLOCK, VIDEO))
        return attend(query_rows, video_keys, video_values, allowed)

    attn_audio = lax.map(audio_rows, jnp.arange(AUDIO // BLOCK, dtype=jnp.int32)).reshape(AUDIO, HD)
    video_out = jnp.dot(attn_video, wo_video, preferred_element_type=jnp.float32).astype(jnp.bfloat16)
    audio_out = jnp.dot(attn_audio, wo_audio, preferred_element_type=jnp.float32).astype(jnp.bfloat16)
    return video_out, audio_out
```

```python
import math

import jax
import jax.numpy as jnp
from jax import lax
from jax.experimental import pallas as pl
from jax.experimental.pallas import tpu as pltpu
from jax.sharding import PartitionSpec as P

MESH = pl.DeviceIdType.MESH
HDIM = 128
BLOCK = 128
NEG = -1e30
BF = jnp.bfloat16
F32 = jnp.float32
SCALE = HDIM ** (-0.5) * math.log2(math.e)

COPIES = 64


def dot(a, b):
    return jnp.dot(a, b, preferred_element_type=F32)


def dot_t(a, b):
    return lax.dot_general(a, b, (((1,), (1,)), ((), ())), preferred_element_type=F32)


def split3(value):
    hi = value.astype(BF).astype(F32)
    rest = value - hi
    mid = rest.astype(BF).astype(F32)
    return hi, mid, rest - mid


def pack_stats(stats, rows):
    lane = lax.broadcasted_iota(jnp.int32, (rows, 128), 1)
    out = jnp.zeros((rows, 128), F32)
    at = 0
    for value in stats:
        for part in split3(value):
            out = jnp.where(lane == at, part, out)
            at += 1
    return out.astype(BF)


def unpack_stat(tile, at):
    return tile[:, at : at + 1] + tile[:, at + 1 : at + 2] + tile[:, at + 2 : at + 3]


def merge(packed, heads):
    peaks, sums, accs = [], [], []
    for hh in range(heads):
        ms = [unpack_stat(tile, hh * 6) for tile, _ in packed]
        ls = [unpack_stat(tile, hh * 6 + 3) for tile, _ in packed]
        peak = ms[0]
        for m in ms[1:]:
            peak = jnp.maximum(peak, m)
        total, acc = 0.0, 0.0
        for m, l, (_, a) in zip(ms, ls, packed):
            w = jnp.exp2(m - peak)
            total = total + w * l
            acc = acc + w * a[hh]
        peaks.append(peak)
        sums.append(total)
        accs.append(acc)
    return peaks, sums, accs


def kernel(
    x_hbm, xa_hbm, kv_hbm, akv_hbm, wq_hbm, wo_hbm, wqa_hbm, woa_hbm, bl, vlen, alen,
    outv, outa,
    X, XA, kvraw, VK, akraw, KW, QW, WQ, WQA, WOC, WOAC, ATT, ATTA,
    SBA, RBA, OWNA, PS, PR, SX, RX, KS, lsem, ssem, rsem,
):
    width = WQ.shape[1]
    heads = width // HDIM
    feat = x_hbm.shape[1]
    arows = xa_hbm.shape[0]
    v = lax.axis_index("vid")
    t = lax.axis_index("tp")
    y = lax.rem(v, 4)
    row = lax.div(v, 4)
    h = lax.div(y, 2)
    c = lax.rem(t, 2)
    zl = lax.div(t, 2)
    tz = lax.rem(t + 2, 4)
    tc = t + 1 - 2 * c
    y1, y2, y3 = y + 1 - 2 * lax.rem(y, 2), lax.rem(y + 2, 4), 3 - y
    nz, nc = (v, tz), (v, tc)
    vo = lax.rem(v + 64 + 16 * (2 * zl - 1), 64)
    td = lax.rem(tc + 2, 4)
    no, nd = (vo, tz), (vo, td)
    plane = lax.div(v, 16) * 16
    x = lax.div(v - plane, 4)
    nxr, nxl = (plane + lax.rem(v - plane + 4, 16), t), (plane + lax.rem(v - plane + 12, 16), t)
    ny1, ny2, ny3 = (row * 4 + y1, t), (row * 4 + y2, t), (row * 4 + y3, t)
    nup, ndn = (lax.rem(v + 4, 64), t), (lax.rem(v + 60, 64), t)

    local = {}

    def load(name, i, src, dst):
        local[name] = pltpu.make_async_copy(src, dst, lsem.at[i])
        local[name].start()

    def cols(i, n):
        return pl.ds(pl.multiple_of(i * n, n), n)

    def shard(i):
        return pl.ds(pl.multiple_of(i * arows, arows), arows)

    load("ak", 0, akv_hbm, akraw)
    load("xa", 1, xa_hbm, XA.at[:, cols(t, feat)])
    load("x", 2, x_hbm, X.at[:, cols(t, feat)])
    load("wqa", 3, wqa_hbm, WQA)
    load("wq", 4, wq_hbm, WQ)
    load("kv", 5, kv_hbm, kvraw)
    orow = pl.ds(pl.multiple_of(c * width, width), width)
    load("wo", 6, wo_hbm.at[:, cols(t, feat)], WOC.at[cols(t, width), :])
    load("wa0", 7, woa_hbm.at[:, cols(zl * 2 + c, feat)], WOAC.at[orow, pl.ds(0, feat)])
    load("wa1", 8, woa_hbm.at[:, cols((1 - zl) * 2 + c, feat)], WOAC.at[orow, pl.ds(feat, feat)])

    barrier = pltpu.get_barrier_semaphore()
    for peer in (nz, nc, ny1, ny2, ny3, nup, ndn, no, nd, nxr, nxl):
        pl.semaphore_signal(barrier, inc=1, device_id=peer, device_id_type=MESH)
    own, lower, upper = 4 + y, y, 8 + y
    sel = y + 8 * (1 - h)
    local["ak"].wait()
    KW[own] = akraw[...].reshape(arows, 2 * width)
    pl.semaphore_wait(barrier, 11)

    sent = {}

    def send(name, src, dst, peer):
        i = len(sent)
        sent[name] = pltpu.make_async_remote_copy(
            src_ref=src, dst_ref=dst, send_sem=ssem.at[i], recv_sem=rsem.at[i],
            device_id=peer, device_id_type=MESH,
        )
        sent[name].start()

    def got(*names):
        for name in names:
            sent[name].wait_recv()

    tcols, zcols = cols(t, feat), cols(tz, feat)

    def send_x(i):
        rows = pl.ds(i * BLOCK, BLOCK)
        send(f"xz{i}", x_hbm.at[rows, :], X.at[rows, tcols], nz)

    def spread_x(p, buf):
        send(p + "up", buf.at[own], buf.at[lower], nup)
        send(p + "dn", buf.at[own], buf.at[upper], ndn)

    def spread_y(p, buf):
        send(p + "y1", buf.at[own], buf.at[own], ny1)
        send(p + "y2", buf.at[own], buf.at[own], ny2)
        send(p + "y3", buf.at[own], buf.at[own], ny3)

    def spread_on(p, buf):
        got(p + "up", p + "dn")
        send(p + "f1a", buf.at[lower], buf.at[lower], ny1)
        send(p + "f1b", buf.at[upper], buf.at[upper], ny1)
        send(p + "f2", buf.at[sel], buf.at[sel], ny2)
        send(p + "f3", buf.at[sel], buf.at[sel], ny3)

    def spread_end(p):
        got(*(p + s for s in ("y1", "y2", "y3", "f1a", "f1b", "f2", "f3")))

    spread_x("k", KW)
    send("xaz", xa_hbm, XA.at[:, tcols], nz)
    send("xac", xa_hbm, XA.at[:, tcols], nc)
    send_x(0)
    spread_y("k", KW)
    send("xc", x_hbm, X.at[:, tcols], nc)

    send("woc", wo_hbm.at[:, cols(tc, feat)], WOC.at[cols(t, width), :], nc)
    part4 = width // 4

    def quarter(to, at):
        return pl.ds(pl.multiple_of(to * width + at * part4, part4), part4)

    for name, to, peer in (("woo", tz, no), ("wod", td, nd)):
        send(name, wo_hbm.at[pl.ds(pl.multiple_of(x * part4, part4), part4), cols(to, feat)],
             WOC.at[quarter(t, x), :], peer)

    def wring1():
        got("woo", "wod")
        for tag, to in (("a", tz), ("b", td)):
            rows = quarter(to, x)
            send("wr" + tag, WOC.at[rows, :], WOC.at[rows, :], nxr)
            send("wl" + tag, WOC.at[rows, :], WOC.at[rows, :], nxl)

    def wring2():
        got("wra", "wrb", "wla", "wlb")
        rows = quarter(tz, lax.rem(x + 3, 4))
        send("wr2", WOC.at[rows, :], WOC.at[rows, :], nxr)
        rows = quarter(td, lax.rem(x + 1, 4))
        send("wl2", WOC.at[rows, :], WOC.at[rows, :], nxl)

    send("wa0", woa_hbm.at[:, cols(zl * 2 + 1 - c, feat)], WOAC.at[orow, pl.ds(0, feat)], nc)
    send("wa1", woa_hbm.at[:, cols((1 - zl) * 2 + 1 - c, feat)], WOAC.at[orow, pl.ds(feat, feat)], nc)

    local["kv"].wait()
    VK[...] = kvraw[...].reshape(kvraw.shape[0], 2 * width)

    def v1(i):
        rows = pl.ds(i * BLOCK, BLOCK)
        got(f"xz{i}")
        send(f"xf{i}", X.at[rows, zcols], X.at[rows, zcols], nc)

    lane = lax.broadcasted_iota(jnp.int32, (1, BLOCK), 1)

    def v2(i):
        rows = pl.ds(i * BLOCK, BLOCK)
        vb = v * 4 + i
        entries = [bl[k, vb] for k in range(3)]
        doubles = [None, entries[1] == entries[0],
                   (entries[2] == entries[0]) | (entries[2] == entries[1])]
        bias = []
        for k in range(3):
            slot = jnp.clip(entries[k] - 2 * row + 2, 0, 5)
            for half in range(2):
                KS[pl.ds(k * BLOCK + half * arows, arows), :] = KW[slot * 2 + half]
            limit = alen[0] - entries[k] * BLOCK
            if k:
                limit = jnp.where(doubles[k], 0, limit)
            bias.append(jnp.where(lane < limit, 0.0, NEG))
        bias = jnp.concatenate(bias, axis=1)
        got(f"xf{i}")
        q = dot(X[rows, :], WQ[...]).astype(BF)
        for hh in range(heads):
            hc = pl.ds(hh * HDIM, HDIM)
            s = dot_t(q[:, hh * HDIM : (hh + 1) * HDIM], KS[:, hc]) * SCALE + bias
            e = jnp.exp2(s - jnp.max(s, axis=1, keepdims=True))
            total = jnp.sum(e, axis=1, keepdims=True)
            acc = dot(e.astype(BF), KS[:, pl.ds(width + hh * HDIM, HDIM)])
            ATT[rows, pl.ds(pl.multiple_of(t * width + hh * HDIM, HDIM), HDIM)] = (
                acc / total
            ).astype(BF)
        mine = cols(t, width)
        send(f"az{i}", ATT.at[rows, mine], ATT.at[rows, mine], nz)
        send(f"ac{i}", ATT.at[rows, mine], ATT.at[rows, mine], nc)

    def v3(i):
        rows = pl.ds(i * BLOCK, BLOCK)
        other = cols(tz, width)
        got(f"az{i}")
        send(f"af{i}", ATT.at[rows, other], ATT.at[rows, other], nc)

    def v4(i):
        rows = pl.ds(i * BLOCK, BLOCK)
        got(f"ac{i}", f"af{i}")
        outv[rows, :] = dot(ATT[rows, :], WOC[...]).astype(BF)

    def a4():
        base = v * 4

        def block(j, _):
            g = h + j
            blk = 2 * row - 2 + g
            bias = []
            for k in range(4):
                vb = base + k
                linked = (bl[0, vb] == blk) | (bl[1, vb] == blk) | (bl[2, vb] == blk)
                limit = jnp.where(linked, vlen[0] - vb * BLOCK, 0)
                bias.append(jnp.where(lane < limit, 0.0, NEG))
            bias = jnp.concatenate(bias, axis=1)
            rows = pl.ds(pl.multiple_of(g * BLOCK, BLOCK), BLOCK)
            stats = []
            qs = jnp.concatenate([QW[2 * g], QW[2 * g + 1]], axis=0)
            for hh in range(heads):
                hc = pl.ds(hh * HDIM, HDIM)
                s = dot_t(qs[:, hh * HDIM : (hh + 1) * HDIM], VK[:, hc]) * SCALE + bias
                m = jnp.max(s, axis=1, keepdims=True)
                e = jnp.exp2(s - m)
                stats += [m, jnp.sum(e, axis=1, keepdims=True)]
                PS[rows, hc] = dot(e.astype(BF), VK[:, pl.ds(width + hh * HDIM, HDIM)]).astype(BF)
            PS[rows, pl.ds(width, 128)] = pack_stats(stats, BLOCK)
            return 0

        lax.fori_loop(0, 5, block, 0)
        for k, yk, peer in ((1, y1, ny1), (2, y2, ny2), (3, y3, ny3)):
            if k == 1:
                parts = (("a", yk, 0), ("b", 4 + yk, 1), ("c", 8 + yk, 2))
            else:
                parts = (("a", 4 + yk, 0), ("b", yk + 8 * h, 1))
            for tag, index, slot in parts:
                send(f"p{k}{tag}", PS.at[shard(index), :],
                     PR.at[pl.ds((k * 3 + slot) * arows, arows), :], peer)

    def part(buf, index):
        rows = shard(index)
        return (
            buf[rows, pl.ds(width, 128)].astype(F32),
            [buf[rows, pl.ds(hh * HDIM, HDIM)].astype(F32) for hh in range(heads)],
        )

    def put(index, state):
        rows = shard(index)
        peaks, sums, accs = state
        stats = []
        for hh in range(heads):
            SX[rows, pl.ds(hh * HDIM, HDIM)] = accs[hh].astype(BF)
            stats += [peaks[hh], sums[hh]]
        SX[rows, pl.ds(width, 128)] = pack_stats(stats, arows)

    def a5():
        got("p1a", "p1b", "p1c", "p2a", "p2b", "p3a", "p3b")
        put(1 - h, merge([part(PS, y + 8 * (1 - h)), part(PR, 3 + 2 * (1 - h)),
                          part(PR, 7), part(PR, 10)], heads))
        put(h, merge([part(PS, y + 8 * h), part(PR, 3 + 2 * h)], heads))
        send("pup", SX.at[pl.ds(arows, arows), :], RX.at[pl.ds(0, arows), :], nup)
        send("pdn", SX.at[pl.ds(0, arows), :], RX.at[pl.ds(arows, arows), :], ndn)

    def a6():
        got("pup", "pdn")
        _, sums, accs = merge(
            [part(PS, 4 + y), part(PR, 4), part(PR, 6), part(PR, 9), part(RX, 0), part(RX, 1)], heads
        )
        for hh in range(heads):
            ATTA[:, pl.ds(pl.multiple_of(c * width + hh * HDIM, HDIM), HDIM)] = (
                accs[hh] / sums[hh]
            ).astype(BF)
        mine = cols(c, width)
        send("ata", ATTA.at[:, mine], ATTA.at[:, mine], nc)

    got("xaz")
    send("xaf", XA.at[:, zcols], XA.at[:, zcols], nc)
    spread_on("k", KW)
    local["xa"].wait()
    local["wqa"].wait()
    got("xac", "xaf")
    QW[own] = dot(XA[...], WQA[...]).astype(BF)
    spread_x("q", QW)
    for i in range(1, 4):
        send_x(i)
    spread_y("q", QW)
    v1(0)
    wring1()
    spread_on("q", QW)
    local["x"].wait()
    local["wq"].wait()
    got("xc")
    spread_end("k")
    v2(0)
    v1(1)
    wring2()
    spread_end("q")
    a4()
    v2(1)
    v1(2)
    v3(0)
    v2(2)
    a5()
    v1(3)
    v3(1)
    v2(3)
    a6()
    v3(2)
    for name in ("wa0", "wa1"):
        local[name].wait()
        got(name)
    got("ata")
    att = ATTA[...]
    SBA[...] = dot(att, WOAC[:, feat:]).astype(BF)
    send("oza", SBA, RBA, nz)
    OWNA[...] = dot(att, WOAC[:, :feat])
    local["wo"].wait()
    got("woc", "wr2", "wl2")
    v3(3)
    for i in range(4):
        v4(i)
    got("oza")
    outa[...] = (OWNA[...] + RBA[...].astype(F32)).astype(BF)
    assert len(sent) == COPIES
    for copy in sent.values():
        copy.wait_send()


def finish(video, audio, outv, outa):
    outv[...] = video[...]
    outa[...] = audio[...]


def per_device(
    video_x, audio_x, video_kv, audio_kv, wq_video, wo_video, wq_audio, wo_audio,
    block_list, video_len, audio_len,
):
    vrows, feat = video_x.shape
    arows = audio_x.shape[0]
    full, width = wq_video.shape
    any_spec = pl.BlockSpec(memory_space=pl.ANY)
    smem = pl.BlockSpec(memory_space=pltpu.SMEM)
    vmem = pl.BlockSpec(memory_space=pltpu.VMEM)

    def V(*shape, dtype=BF):
        return pltpu.VMEM(shape, dtype)

    outs = pl.pallas_call(
        kernel,
        out_shape=[
            jax.ShapeDtypeStruct((vrows, feat), BF),
            jax.ShapeDtypeStruct((arows, feat), BF),
        ],
        in_specs=[any_spec] * 8 + [smem] * 3,
        out_specs=[vmem] * 2,
        scratch_shapes=[
            V(vrows, full), V(arows, full),
            V(vrows, 2, width), V(vrows, 2 * width), V(arows, 2, width),
            V(12, arows, 2 * width), V(12, arows, width),
            V(full, width), V(full, width), V(4 * width, feat), V(2 * width, 2 * feat),
            V(vrows, 4 * width), V(arows, 2 * width),
            V(arows, feat), V(arows, feat), V(arows, feat, dtype=F32),
            V(12 * arows, width + 128), V(12 * arows, width + 128),
            V(2 * arows, width + 128), V(2 * arows, width + 128),
            V(3 * BLOCK, 2 * width),
            pltpu.SemaphoreType.DMA((9,)),
            pltpu.SemaphoreType.DMA((COPIES,)),
            pltpu.SemaphoreType.DMA((COPIES,)),
        ],
        compiler_params=pltpu.CompilerParams(
            collective_id=0, has_side_effects=True, vmem_limit_bytes=56 * 2**20
        ),
        cost_estimate=pl.CostEstimate(
            flops=4_000_000_000, bytes_accessed=14_000_000, transcendentals=2_000_000
        ),
        name="twin_tower",
    )(
        video_x, audio_x, video_kv, audio_kv, wq_video, wo_video, wq_audio, wo_audio,
        block_list.T, video_len, audio_len,
    )
    return pl.pallas_call(
        finish,
        out_shape=[jax.ShapeDtypeStruct(o.shape, o.dtype) for o in outs],
        in_specs=[vmem] * 2,
        out_specs=[vmem] * 2,
        name="finish",
    )(*outs)


def solution(mesh):
    in_specs = (
        P("vid", "tp"), P("vid", "tp"), P("vid", None, "tp"), P("vid", None, "tp"),
        P(None, "tp"), P("tp", None), P(None, "tp"), P("tp", None), P(), P(), P(),
    )
    return jax.shard_map(
        per_device, mesh=mesh, in_specs=in_specs, out_specs=(P("vid", "tp"), P("vid", "tp")),
        check_vma=False,
    )
```

```python
import math

import jax
import jax.numpy as jnp
from jax import lax
from jax.experimental import pallas as pl
from jax.experimental.pallas import tpu as pltpu
from jax.sharding import PartitionSpec as P

MESH = pl.DeviceIdType.MESH
HDIM = 128
BLOCK = 128
NEG = -1e30
BF = jnp.bfloat16
F32 = jnp.float32
SCALE = HDIM ** (-0.5) * math.log2(math.e)

COPIES = 64


def dot(a, b):
    return jnp.dot(a, b, preferred_element_type=F32)


def dot_t(a, b):
    return lax.dot_general(a, b, (((1,), (1,)), ((), ())), preferred_element_type=F32)


def split3(value):
    hi = value.astype(BF).astype(F32)
    rest = value - hi
    mid = rest.astype(BF).astype(F32)
    return hi, mid, rest - mid


def pack_stats(stats, rows):
    lane = lax.broadcasted_iota(jnp.int32, (rows, 128), 1)
    out = jnp.zeros((rows, 128), F32)
    at = 0
    for value in stats:
        for part in split3(value):
            out = jnp.where(lane == at, part, out)
            at += 1
    return out.astype(BF)


def unpack_stat(tile, at):
    return tile[:, at : at + 1] + tile[:, at + 1 : at + 2] + tile[:, at + 2 : at + 3]


def merge(packed, heads):
    peaks, sums, accs = [], [], []
    for hh in range(heads):
        ms = [unpack_stat(tile, hh * 6) for tile, _ in packed]
        ls = [unpack_stat(tile, hh * 6 + 3) for tile, _ in packed]
        peak = ms[0]
        for m in ms[1:]:
            peak = jnp.maximum(peak, m)
        total, acc = 0.0, 0.0
        for m, l, (_, a) in zip(ms, ls, packed):
            w = jnp.exp2(m - peak)
            total = total + w * l
            acc = acc + w * a[hh]
        peaks.append(peak)
        sums.append(total)
        accs.append(acc)
    return peaks, sums, accs


def kernel(
    x_hbm, xa_hbm, kv_hbm, akv_hbm, wq_hbm, wo_hbm, wqa_hbm, woa_hbm, bl_hbm, vlen_hbm, alen_hbm,
    outv, outa,
    X, XA, kvraw, VK, akraw, KW, QW, WQ, WQA, WOC, WOAC, ATT, ATTA,
    SBA, RBA, OWNA, PS, PR, SX, RX, KS, bl, vlen, alen, lsem, ssem, rsem,
):
    width = WQ.shape[1]
    heads = width // HDIM
    feat = x_hbm.shape[1]
    arows = xa_hbm.shape[0]
    v = lax.axis_index("vid")
    t = lax.axis_index("tp")
    y = lax.rem(v, 4)
    row = lax.div(v, 4)
    h = lax.div(y, 2)
    c = lax.rem(t, 2)
    zl = lax.div(t, 2)
    tz = lax.rem(t + 2, 4)
    tc = t + 1 - 2 * c
    y1, y2, y3 = y + 1 - 2 * lax.rem(y, 2), lax.rem(y + 2, 4), 3 - y
    nz, nc = (v, tz), (v, tc)
    vo = lax.rem(v + 64 + 16 * (2 * zl - 1), 64)
    td = lax.rem(tc + 2, 4)
    no, nd = (vo, tz), (vo, td)
    plane = lax.div(v, 16) * 16
    x = lax.div(v - plane, 4)
    nxr, nxl = (plane + lax.rem(v - plane + 4, 16), t), (plane + lax.rem(v - plane + 12, 16), t)
    ny1, ny2, ny3 = (row * 4 + y1, t), (row * 4 + y2, t), (row * 4 + y3, t)
    nup, ndn = (lax.rem(v + 4, 64), t), (lax.rem(v + 60, 64), t)

    local = {}

    def load(name, i, src, dst):
        local[name] = pltpu.make_async_copy(src, dst, lsem.at[i])
        local[name].start()

    def cols(i, n):
        return pl.ds(pl.multiple_of(i * n, n), n)

    def shard(i):
        return pl.ds(pl.multiple_of(i * arows, arows), arows)

    load("ak", 0, akv_hbm, akraw)
    load("bl", 9, bl_hbm, bl)
    load("vlen", 10, vlen_hbm, vlen)
    load("alen", 11, alen_hbm, alen)
    load("xa", 1, xa_hbm, XA.at[:, cols(t, feat)])
    load("x", 2, x_hbm, X.at[:, cols(t, feat)])
    load("wqa", 3, wqa_hbm, WQA)
    load("wq", 4, wq_hbm, WQ)
    load("kv", 5, kv_hbm, kvraw)
    orow = pl.ds(pl.multiple_of(c * width, width), width)
    load("wo", 6, wo_hbm.at[:, cols(t, feat)], WOC.at[cols(t, width), :])
    load("wa0", 7, woa_hbm.at[:, cols(zl * 2 + c, feat)], WOAC.at[orow, pl.ds(0, feat)])
    load("wa1", 8, woa_hbm.at[:, cols((1 - zl) * 2 + c, feat)], WOAC.at[orow, pl.ds(feat, feat)])

    barrier = pltpu.get_barrier_semaphore()
    for peer in (nz, nc, ny1, ny2, ny3, nup, ndn, no, nd, nxr, nxl):
        pl.semaphore_signal(barrier, inc=1, device_id=peer, device_id_type=MESH)
    own, lower, upper = 4 + y, y, 8 + y
    sel = y + 8 * (1 - h)
    local["ak"].wait()
    KW[own] = akraw[...].reshape(arows, 2 * width)
    pl.semaphore_wait(barrier, 11)

    sent = {}

    def send(name, src, dst, peer):
        i = len(sent)
        sent[name] = pltpu.make_async_remote_copy(
            src_ref=src, dst_ref=dst, send_sem=ssem.at[i], recv_sem=rsem.at[i],
            device_id=peer, device_id_type=MESH,
        )
        sent[name].start()

    def got(*names):
        for name in names:
            sent[name].wait_recv()

    tcols, zcols = cols(t, feat), cols(tz, feat)

    def send_x(i):
        rows = pl.ds(i * BLOCK, BLOCK)
        send(f"xz{i}", x_hbm.at[rows, :], X.at[rows, tcols], nz)

    def spread_x(p, buf):
        send(p + "up", buf.at[own], buf.at[lower], nup)
        send(p + "dn", buf.at[own], buf.at[upper], ndn)

    def spread_y(p, buf):
        send(p + "y1", buf.at[own], buf.at[own], ny1)
        send(p + "y2", buf.at[own], buf.at[own], ny2)
        send(p + "y3", buf.at[own], buf.at[own], ny3)

    def spread_on(p, buf):
        got(p + "up", p + "dn")
        send(p + "f1a", buf.at[lower], buf.at[lower], ny1)
        send(p + "f1b", buf.at[upper], buf.at[upper], ny1)
        send(p + "f2", buf.at[sel], buf.at[sel], ny2)
        send(p + "f3", buf.at[sel], buf.at[sel], ny3)

    def spread_end(p):
        got(*(p + s for s in ("y1", "y2", "y3", "f1a", "f1b", "f2", "f3")))

    send("xaz", xa_hbm, XA.at[:, tcols], nz)
    send("xac", xa_hbm, XA.at[:, tcols], nc)
    spread_x("k", KW)
    send_x(0)
    spread_y("k", KW)
    send("xc", x_hbm, X.at[:, tcols], nc)

    send("woc", wo_hbm.at[:, cols(tc, feat)], WOC.at[cols(t, width), :], nc)
    part4 = width // 4

    def quarter(to, at):
        return pl.ds(pl.multiple_of(to * width + at * part4, part4), part4)

    for name, to, peer in (("woo", tz, no), ("wod", td, nd)):
        send(name, wo_hbm.at[pl.ds(pl.multiple_of(x * part4, part4), part4), cols(to, feat)],
             WOC.at[quarter(t, x), :], peer)

    def wring1():
        got("woo", "wod")
        for tag, to in (("a", tz), ("b", td)):
            rows = quarter(to, x)
            send("wr" + tag, WOC.at[rows, :], WOC.at[rows, :], nxr)
            send("wl" + tag, WOC.at[rows, :], WOC.at[rows, :], nxl)

    def wring2():
        got("wra", "wrb", "wla", "wlb")
        rows = quarter(tz, lax.rem(x + 3, 4))
        send("wr2", WOC.at[rows, :], WOC.at[rows, :], nxr)
        rows = quarter(td, lax.rem(x + 1, 4))
        send("wl2", WOC.at[rows, :], WOC.at[rows, :], nxl)

    send("wa0", woa_hbm.at[:, cols(zl * 2 + 1 - c, feat)], WOAC.at[orow, pl.ds(0, feat)], nc)
    send("wa1", woa_hbm.at[:, cols((1 - zl) * 2 + 1 - c, feat)], WOAC.at[orow, pl.ds(feat, feat)], nc)

    local["kv"].wait()
    VK[...] = kvraw[...].reshape(kvraw.shape[0], 2 * width)

    def v1(i):
        rows = pl.ds(i * BLOCK, BLOCK)
        got(f"xz{i}")
        send(f"xf{i}", X.at[rows, zcols], X.at[rows, zcols], nc)

    lane = lax.broadcasted_iota(jnp.int32, (1, BLOCK), 1)

    def v2(i):
        rows = pl.ds(i * BLOCK, BLOCK)
        vb = v * 4 + i
        entries = [bl[k, vb] for k in range(3)]
        doubles = [None, entries[1] == entries[0],
                   (entries[2] == entries[0]) | (entries[2] == entries[1])]
        bias = []
        for k in range(3):
            slot = jnp.clip(entries[k] - 2 * row + 2, 0, 5)
            for half in range(2):
                KS[pl.ds(k * BLOCK + half * arows, arows), :] = KW[slot * 2 + half]
            limit = alen[0] - entries[k] * BLOCK
            if k:
                limit = jnp.where(doubles[k], 0, limit)
            bias.append(jnp.where(lane < limit, 0.0, NEG))
        bias = jnp.concatenate(bias, axis=1)
        got(f"xf{i}")
        q = dot(X[rows, :], WQ[...]).astype(BF)
        for hh in range(heads):
            hc = pl.ds(hh * HDIM, HDIM)
            s = dot_t(q[:, hh * HDIM : (hh + 1) * HDIM], KS[:, hc]) * SCALE + bias
            e = jnp.exp2(s - jnp.max(s, axis=1, keepdims=True))
            total = jnp.sum(e, axis=1, keepdims=True)
            acc = dot(e.astype(BF), KS[:, pl.ds(width + hh * HDIM, HDIM)])
            ATT[rows, pl.ds(pl.multiple_of(t * width + hh * HDIM, HDIM), HDIM)] = (
                acc / total
            ).astype(BF)
        mine = cols(t, width)
        send(f"az{i}", ATT.at[rows, mine], ATT.at[rows, mine], nz)
        send(f"ac{i}", ATT.at[rows, mine], ATT.at[rows, mine], nc)

    def v3(i):
        rows = pl.ds(i * BLOCK, BLOCK)
        other = cols(tz, width)
        got(f"az{i}")
        send(f"af{i}", ATT.at[rows, other], ATT.at[rows, other], nc)

    def v4(i):
        rows = pl.ds(i * BLOCK, BLOCK)
        got(f"ac{i}", f"af{i}")
        outv[rows, :] = dot(ATT[rows, :], WOC[...]).astype(BF)

    def a4():
        base = v * 4

        def block(j):
            g = h + j
            blk = 2 * row - 2 + g
            bias = []
            for k in range(4):
                vb = base + k
                linked = (bl[0, vb] == blk) | (bl[1, vb] == blk) | (bl[2, vb] == blk)
                limit = jnp.where(linked, vlen[0] - vb * BLOCK, 0)
                bias.append(jnp.where(lane < limit, 0.0, NEG))
            bias = jnp.concatenate(bias, axis=1)
            rows = pl.ds(pl.multiple_of(g * BLOCK, BLOCK), BLOCK)
            stats = []
            qs = jnp.concatenate([QW[2 * g], QW[2 * g + 1]], axis=0)
            for hh in range(heads):
                hc = pl.ds(hh * HDIM, HDIM)
                s = dot_t(qs[:, hh * HDIM : (hh + 1) * HDIM], VK[:, hc]) * SCALE + bias
                m = jnp.max(s, axis=1, keepdims=True)
                e = jnp.exp2(s - m)
                stats += [m, jnp.sum(e, axis=1, keepdims=True)]
                PS[rows, hc] = dot(e.astype(BF), VK[:, pl.ds(width + hh * HDIM, HDIM)]).astype(BF)
            PS[rows, pl.ds(width, 128)] = pack_stats(stats, BLOCK)

        def give(name, index, slot, peer):
            send(name, PS.at[shard(index), :], PR.at[pl.ds(slot * arows, arows), :], peer)

        for j in (1, 3):
            block(j)
        give("p2a", 4 + y2, 6, ny2)
        give("p3a", 4 + y3, 9, ny3)
        give("p2b", y2 + 8 * h, 7, ny2)
        give("p3b", y3 + 8 * h, 10, ny3)
        block(0)
        give("p1a", y1, 3, ny1)
        block(4)
        give("p1c", 8 + y1, 5, ny1)
        block(2)
        give("p1b", 4 + y1, 4, ny1)

    def part(buf, index):
        rows = shard(index)
        return (
            buf[rows, pl.ds(width, 128)].astype(F32),
            [buf[rows, pl.ds(hh * HDIM, HDIM)].astype(F32) for hh in range(heads)],
        )

    def put(index, state):
        rows = shard(index)
        peaks, sums, accs = state
        stats = []
        for hh in range(heads):
            SX[rows, pl.ds(hh * HDIM, HDIM)] = accs[hh].astype(BF)
            stats += [peaks[hh], sums[hh]]
        SX[rows, pl.ds(width, 128)] = pack_stats(stats, arows)

    def a5():
        got("p1a", "p1b", "p1c", "p2a", "p2b", "p3a", "p3b")
        put(1 - h, merge([part(PS, y + 8 * (1 - h)), part(PR, 3 + 2 * (1 - h)),
                          part(PR, 7), part(PR, 10)], heads))
        put(h, merge([part(PS, y + 8 * h), part(PR, 3 + 2 * h)], heads))
        send("pup", SX.at[pl.ds(arows, arows), :], RX.at[pl.ds(0, arows), :], nup)
        send("pdn", SX.at[pl.ds(0, arows), :], RX.at[pl.ds(arows, arows), :], ndn)

    def a6():
        got("pup", "pdn")
        _, sums, accs = merge(
            [part(PS, 4 + y), part(PR, 4), part(PR, 6), part(PR, 9), part(RX, 0), part(RX, 1)], heads
        )
        for hh in range(heads):
            ATTA[:, pl.ds(pl.multiple_of(c * width + hh * HDIM, HDIM), HDIM)] = (
                accs[hh] / sums[hh]
            ).astype(BF)
        mine = cols(c, width)
        send("ata", ATTA.at[:, mine], ATTA.at[:, mine], nc)

    for name in ("bl", "vlen", "alen"):
        local[name].wait()
    got("xaz")
    send("xaf", XA.at[:, zcols], XA.at[:, zcols], nc)
    local["xa"].wait()
    local["wqa"].wait()
    got("xac", "xaf")
    QW[own] = dot(XA[...], WQA[...]).astype(BF)
    spread_x("q", QW)
    send_x(1)
    spread_y("q", QW)
    spread_on("q", QW)
    send_x(2)
    send_x(3)
    spread_on("k", KW)
    wring1()
    v1(0)
    spread_end("q")
    a4()
    v1(1)
    wring2()
    local["x"].wait()
    local["wq"].wait()
    got("xc")
    spread_end("k")
    v2(0)
    v1(2)
    a5()
    v2(1)
    v3(0)
    v2(2)
    v1(3)
    a6()
    v3(1)
    v2(3)
    for name in ("wa0", "wa1"):
        local[name].wait()
        got(name)
    got("ata")
    att = ATTA[...]
    SBA[...] = dot(att, WOAC[:, feat:]).astype(BF)
    send("oza", SBA, RBA, nz)
    OWNA[...] = dot(att, WOAC[:, :feat])
    local["wo"].wait()
    got("woc", "wr2", "wl2")
    v3(2)
    v4(0)
    v3(3)
    for i in range(1, 4):
        v4(i)
    got("oza")
    outa[...] = (OWNA[...] + RBA[...].astype(F32)).astype(BF)
    assert len(sent) == COPIES
    for copy in sent.values():
        copy.wait_send()


def finish(video, audio, outv, outa):
    outv[...] = video[...]
    outa[...] = audio[...]


def per_device(
    video_x, audio_x, video_kv, audio_kv, wq_video, wo_video, wq_audio, wo_audio,
    block_list, video_len, audio_len,
):
    vrows, feat = video_x.shape
    arows = audio_x.shape[0]
    full, width = wq_video.shape
    any_spec = pl.BlockSpec(memory_space=pl.ANY)
    vmem = pl.BlockSpec(memory_space=pltpu.VMEM)

    def V(*shape, dtype=BF):
        return pltpu.VMEM(shape, dtype)

    outs = pl.pallas_call(
        kernel,
        out_shape=[
            jax.ShapeDtypeStruct((vrows, feat), BF),
            jax.ShapeDtypeStruct((arows, feat), BF),
        ],
        in_specs=[any_spec] * 11,
        out_specs=[vmem] * 2,
        scratch_shapes=[
            V(vrows, full), V(arows, full),
            V(vrows, 2, width), V(vrows, 2 * width), V(arows, 2, width),
            V(12, arows, 2 * width), V(12, arows, width),
            V(full, width), V(full, width), V(4 * width, feat), V(2 * width, 2 * feat),
            V(vrows, 4 * width), V(arows, 2 * width),
            V(arows, feat), V(arows, feat), V(arows, feat, dtype=F32),
            V(12 * arows, width + 128), V(12 * arows, width + 128),
            V(2 * arows, width + 128), V(2 * arows, width + 128),
            V(3 * BLOCK, 2 * width),
            pltpu.SMEM(block_list.shape[::-1], jnp.int32), pltpu.SMEM((1,), jnp.int32), pltpu.SMEM((1,), jnp.int32),
            pltpu.SemaphoreType.DMA((12,)),
            pltpu.SemaphoreType.DMA((COPIES,)),
            pltpu.SemaphoreType.DMA((COPIES,)),
        ],
        compiler_params=pltpu.CompilerParams(
            collective_id=0, has_side_effects=True, vmem_limit_bytes=56 * 2**20
        ),
        cost_estimate=pl.CostEstimate(
            flops=4_000_000_000, bytes_accessed=14_000_000, transcendentals=2_000_000
        ),
        name="twin_tower",
    )(
        video_x, audio_x, video_kv, audio_kv, wq_video, wo_video, wq_audio, wo_audio,
        block_list.T, video_len, audio_len,
    )
    return pl.pallas_call(
        finish,
        out_shape=[jax.ShapeDtypeStruct(o.shape, o.dtype) for o in outs],
        in_specs=[vmem] * 2,
        out_specs=[vmem] * 2,
        name="finish",
    )(*outs)


def solution(mesh):
    in_specs = (
        P("vid", "tp"), P("vid", "tp"), P("vid", None, "tp"), P("vid", None, "tp"),
        P(None, "tp"), P("tp", None), P(None, "tp"), P("tp", None), P(), P(), P(),
    )
    return jax.shard_map(
        per_device, mesh=mesh, in_specs=in_specs, out_specs=(P("vid", "tp"), P("vid", "tp")),
        check_vma=False,
    )
```

```python
import math

import jax
import jax.numpy as jnp
from jax import lax
from jax.experimental import pallas as pl
from jax.experimental.pallas import tpu as pltpu
from jax.sharding import PartitionSpec as P

MESH = pl.DeviceIdType.MESH
HDIM = 128
BLOCK = 128
NEG = -1e30
BF = jnp.bfloat16
F32 = jnp.float32
SCALE = HDIM ** (-0.5) * math.log2(math.e)

COPIES = 64


def dot(a, b):
    return jnp.dot(a, b, preferred_element_type=F32)


def dot_t(a, b):
    return lax.dot_general(a, b, (((1,), (1,)), ((), ())), preferred_element_type=F32)


def split3(value):
    hi = value.astype(BF).astype(F32)
    rest = value - hi
    mid = rest.astype(BF).astype(F32)
    return hi, mid, rest - mid


def pack_stats(stats, rows):
    lane = lax.broadcasted_iota(jnp.int32, (rows, 128), 1)
    out = jnp.zeros((rows, 128), F32)
    at = 0
    for value in stats:
        for part in split3(value):
            out = jnp.where(lane == at, part, out)
            at += 1
    return out.astype(BF)


def unpack_stat(tile, at):
    return tile[:, at : at + 1] + tile[:, at + 1 : at + 2] + tile[:, at + 2 : at + 3]


def merge(packed, heads):
    peaks, sums, accs = [], [], []
    for hh in range(heads):
        ms = [unpack_stat(tile, hh * 6) for tile, _ in packed]
        ls = [unpack_stat(tile, hh * 6 + 3) for tile, _ in packed]
        peak = ms[0]
        for m in ms[1:]:
            peak = jnp.maximum(peak, m)
        total, acc = 0.0, 0.0
        for m, l, (_, a) in zip(ms, ls, packed):
            w = jnp.exp2(m - peak)
            total = total + w * l
            acc = acc + w * a[hh]
        peaks.append(peak)
        sums.append(total)
        accs.append(acc)
    return peaks, sums, accs


def kernel(
    x_hbm, xa_hbm, kv_hbm, akv_hbm, wq_hbm, wo_hbm, wqa_hbm, woa_hbm, bl_hbm, vlen_hbm, alen_hbm,
    outv, outa,
    X, XA, kvraw, VK, akraw, KW, QW, WQ, WQA, WOC, WOAC, ATT, ATTA,
    SBA, RBA, OWNA, PS, PR, SX, RX, KS, bl, vlen, alen, lsem, ssem, rsem,
):
    width = WQ.shape[1]
    heads = width // HDIM
    feat = x_hbm.shape[1]
    arows = xa_hbm.shape[0]
    v = lax.axis_index("vid")
    t = lax.axis_index("tp")
    y = lax.rem(v, 4)
    row = lax.div(v, 4)
    h = lax.div(y, 2)
    c = lax.rem(t, 2)
    zl = lax.div(t, 2)
    tz = lax.rem(t + 2, 4)
    tc = t + 1 - 2 * c
    y1, y2, y3 = y + 1 - 2 * lax.rem(y, 2), lax.rem(y + 2, 4), 3 - y
    nz, nc = (v, tz), (v, tc)
    vo = lax.rem(v + 64 + 16 * (2 * zl - 1), 64)
    td = lax.rem(tc + 2, 4)
    no, nd = (vo, tz), (vo, td)
    plane = lax.div(v, 16) * 16
    x = lax.div(v - plane, 4)
    nxr, nxl = (plane + lax.rem(v - plane + 4, 16), t), (plane + lax.rem(v - plane + 12, 16), t)
    ny1, ny2, ny3 = (row * 4 + y1, t), (row * 4 + y2, t), (row * 4 + y3, t)
    nup, ndn = (lax.rem(v + 4, 64), t), (lax.rem(v + 60, 64), t)

    local = {}

    def load(name, i, src, dst):
        local[name] = pltpu.make_async_copy(src, dst, lsem.at[i])
        local[name].start()

    def cols(i, n):
        return pl.ds(pl.multiple_of(i * n, n), n)

    def shard(i):
        return pl.ds(pl.multiple_of(i * arows, arows), arows)

    load("ak", 0, akv_hbm, akraw)
    load("bl", 9, bl_hbm, bl)
    load("vlen", 10, vlen_hbm, vlen)
    load("alen", 11, alen_hbm, alen)
    load("xa", 1, xa_hbm, XA.at[:, cols(t, feat)])
    load("x", 2, x_hbm, X.at[:, cols(t, feat)])
    load("wqa", 3, wqa_hbm, WQA)
    load("wq", 4, wq_hbm, WQ)
    load("kv", 5, kv_hbm, kvraw)
    orow = pl.ds(pl.multiple_of(c * width, width), width)
    load("wo", 6, wo_hbm.at[:, cols(t, feat)], WOC.at[cols(t, width), :])
    load("wa0", 7, woa_hbm.at[:, cols(zl * 2 + c, feat)], WOAC.at[orow, pl.ds(0, feat)])
    load("wa1", 8, woa_hbm.at[:, cols((1 - zl) * 2 + c, feat)], WOAC.at[orow, pl.ds(feat, feat)])

    barrier = pltpu.get_barrier_semaphore()
    for peer in (nz, nc, ny1, ny2, ny3, nup, ndn, no, nd, nxr, nxl):
        pl.semaphore_signal(barrier, inc=1, device_id=peer, device_id_type=MESH)
    own, lower, upper = 4 + y, y, 8 + y
    sel = y + 8 * (1 - h)
    local["ak"].wait()
    KW[own] = akraw[...].reshape(arows, 2 * width)
    pl.semaphore_wait(barrier, 11)

    sent = {}

    def send(name, src, dst, peer):
        i = len(sent)
        sent[name] = pltpu.make_async_remote_copy(
            src_ref=src, dst_ref=dst, send_sem=ssem.at[i], recv_sem=rsem.at[i],
            device_id=peer, device_id_type=MESH,
        )
        sent[name].start()

    def got(*names):
        for name in names:
            sent[name].wait_recv()

    tcols, zcols = cols(t, feat), cols(tz, feat)

    def send_x(i):
        rows = pl.ds(i * BLOCK, BLOCK)
        send(f"xz{i}", x_hbm.at[rows, :], X.at[rows, tcols], nz)

    def spread_x(p, buf):
        send(p + "up", buf.at[own], buf.at[lower], nup)
        send(p + "dn", buf.at[own], buf.at[upper], ndn)

    def spread_y(p, buf):
        send(p + "y1", buf.at[own], buf.at[own], ny1)
        send(p + "y2", buf.at[own], buf.at[own], ny2)
        send(p + "y3", buf.at[own], buf.at[own], ny3)

    def spread_on(p, buf):
        got(p + "up", p + "dn")
        send(p + "f1a", buf.at[lower], buf.at[lower], ny1)
        send(p + "f1b", buf.at[upper], buf.at[upper], ny1)
        send(p + "f2", buf.at[sel], buf.at[sel], ny2)
        send(p + "f3", buf.at[sel], buf.at[sel], ny3)

    def spread_end(p):
        got(*(p + s for s in ("y1", "y2", "y3", "f1a", "f1b", "f2", "f3")))

    send("xaz", xa_hbm, XA.at[:, tcols], nz)
    send("xac", xa_hbm, XA.at[:, tcols], nc)
    spread_x("k", KW)
    send_x(0)
    spread_y("k", KW)
    send("xc", x_hbm, X.at[:, tcols], nc)

    send("woc", wo_hbm.at[:, cols(tc, feat)], WOC.at[cols(t, width), :], nc)
    part4 = width // 4

    def quarter(to, at):
        return pl.ds(pl.multiple_of(to * width + at * part4, part4), part4)

    for name, to, peer in (("woo", tz, no), ("wod", td, nd)):
        send(name, wo_hbm.at[pl.ds(pl.multiple_of(x * part4, part4), part4), cols(to, feat)],
             WOC.at[quarter(t, x), :], peer)

    def wring1():
        got("woo", "wod")
        for tag, to in (("a", tz), ("b", td)):
            rows = quarter(to, x)
            send("wr" + tag, WOC.at[rows, :], WOC.at[rows, :], nxr)
            send("wl" + tag, WOC.at[rows, :], WOC.at[rows, :], nxl)

    def wring2():
        got("wra", "wrb", "wla", "wlb")
        rows = quarter(tz, lax.rem(x + 3, 4))
        send("wr2", WOC.at[rows, :], WOC.at[rows, :], nxr)
        rows = quarter(td, lax.rem(x + 1, 4))
        send("wl2", WOC.at[rows, :], WOC.at[rows, :], nxl)

    send("wa0", woa_hbm.at[:, cols(zl * 2 + 1 - c, feat)], WOAC.at[orow, pl.ds(0, feat)], nc)
    send("wa1", woa_hbm.at[:, cols((1 - zl) * 2 + 1 - c, feat)], WOAC.at[orow, pl.ds(feat, feat)], nc)

    local["kv"].wait()
    VK[...] = kvraw[...].reshape(kvraw.shape[0], 2 * width)

    def v1(i):
        rows = pl.ds(i * BLOCK, BLOCK)
        got(f"xz{i}")
        send(f"xf{i}", X.at[rows, zcols], X.at[rows, zcols], nc)

    lane = lax.broadcasted_iota(jnp.int32, (1, BLOCK), 1)

    def v2(i):
        rows = pl.ds(i * BLOCK, BLOCK)
        vb = v * 4 + i
        entries = [bl[k, vb] for k in range(3)]
        doubles = [None, entries[1] == entries[0],
                   (entries[2] == entries[0]) | (entries[2] == entries[1])]
        bias = []
        for k in range(3):
            slot = jnp.clip(entries[k] - 2 * row + 2, 0, 5)
            for half in range(2):
                KS[pl.ds(k * BLOCK + half * arows, arows), :] = KW[slot * 2 + half]
            limit = alen[0] - entries[k] * BLOCK
            if k:
                limit = jnp.where(doubles[k], 0, limit)
            bias.append(jnp.where(lane < limit, 0.0, NEG))
        bias = jnp.concatenate(bias, axis=1)
        got(f"xf{i}")
        q = dot(X[rows, :], WQ[...]).astype(BF)
        for hh in range(heads):
            hc = pl.ds(hh * HDIM, HDIM)
            s = dot_t(q[:, hh * HDIM : (hh + 1) * HDIM], KS[:, hc]) * SCALE + bias
            e = jnp.exp2(s - jnp.max(s, axis=1, keepdims=True))
            total = jnp.sum(e, axis=1, keepdims=True)
            acc = dot(e.astype(BF), KS[:, pl.ds(width + hh * HDIM, HDIM)])
            ATT[rows, pl.ds(pl.multiple_of(t * width + hh * HDIM, HDIM), HDIM)] = (
                acc / total
            ).astype(BF)
        mine = cols(t, width)
        send(f"az{i}", ATT.at[rows, mine], ATT.at[rows, mine], nz)
        send(f"ac{i}", ATT.at[rows, mine], ATT.at[rows, mine], nc)

    def v3(i):
        rows = pl.ds(i * BLOCK, BLOCK)
        other = cols(tz, width)
        got(f"az{i}")
        send(f"af{i}", ATT.at[rows, other], ATT.at[rows, other], nc)

    def v4(i):
        rows = pl.ds(i * BLOCK, BLOCK)
        got(f"ac{i}", f"af{i}")
        outv[rows, :] = dot(ATT[rows, :], WOC[...]).astype(BF)

    def a4():
        base = v * 4

        def block(j):
            g = h + j
            blk = 2 * row - 2 + g
            bias = []
            for k in range(4):
                vb = base + k
                linked = (bl[0, vb] == blk) | (bl[1, vb] == blk) | (bl[2, vb] == blk)
                limit = jnp.where(linked, vlen[0] - vb * BLOCK, 0)
                bias.append(jnp.where(lane < limit, 0.0, NEG))
            bias = jnp.concatenate(bias, axis=1)
            rows = pl.ds(pl.multiple_of(g * BLOCK, BLOCK), BLOCK)
            stats = []
            qs = jnp.concatenate([QW[2 * g], QW[2 * g + 1]], axis=0)
            for hh in range(heads):
                hc = pl.ds(hh * HDIM, HDIM)
                s = dot_t(qs[:, hh * HDIM : (hh + 1) * HDIM], VK[:, hc]) * SCALE + bias
                m = jnp.max(s, axis=1, keepdims=True)
                e = jnp.exp2(s - m)
                stats += [m, jnp.sum(e, axis=1, keepdims=True)]
                PS[rows, hc] = dot(e.astype(BF), VK[:, pl.ds(width + hh * HDIM, HDIM)]).astype(BF)
            PS[rows, pl.ds(width, 128)] = pack_stats(stats, BLOCK)

        def give(name, index, slot, peer):
            send(name, PS.at[shard(index), :], PR.at[pl.ds(slot * arows, arows), :], peer)

        for j in (1, 3):
            block(j)
        give("p2a", 4 + y2, 6, ny2)
        give("p3a", 4 + y3, 9, ny3)
        give("p2b", y2 + 8 * h, 7, ny2)
        give("p3b", y3 + 8 * h, 10, ny3)
        block(0)
        give("p1a", y1, 3, ny1)
        block(4)
        give("p1c", 8 + y1, 5, ny1)
        block(2)
        give("p1b", 4 + y1, 4, ny1)

    def part(buf, index):
        rows = shard(index)
        return (
            buf[rows, pl.ds(width, 128)].astype(F32),
            [buf[rows, pl.ds(hh * HDIM, HDIM)].astype(F32) for hh in range(heads)],
        )

    def put(index, state):
        rows = shard(index)
        peaks, sums, accs = state
        stats = []
        for hh in range(heads):
            SX[rows, pl.ds(hh * HDIM, HDIM)] = accs[hh].astype(BF)
            stats += [peaks[hh], sums[hh]]
        SX[rows, pl.ds(width, 128)] = pack_stats(stats, arows)

    def a5():
        got("p1a", "p1b", "p1c", "p2a", "p2b", "p3a", "p3b")
        put(1 - h, merge([part(PS, y + 8 * (1 - h)), part(PR, 3 + 2 * (1 - h)),
                          part(PR, 7), part(PR, 10)], heads))
        put(h, merge([part(PS, y + 8 * h), part(PR, 3 + 2 * h)], heads))
        send("pup", SX.at[pl.ds(arows, arows), :], RX.at[pl.ds(0, arows), :], nup)
        send("pdn", SX.at[pl.ds(0, arows), :], RX.at[pl.ds(arows, arows), :], ndn)

    def a6():
        got("pup", "pdn")
        _, sums, accs = merge(
            [part(PS, 4 + y), part(PR, 4), part(PR, 6), part(PR, 9), part(RX, 0), part(RX, 1)], heads
        )
        for hh in range(heads):
            ATTA[:, pl.ds(pl.multiple_of(c * width + hh * HDIM, HDIM), HDIM)] = (
                accs[hh] / sums[hh]
            ).astype(BF)
        mine = cols(c, width)
        send("ata", ATTA.at[:, mine], ATTA.at[:, mine], nc)

    for name in ("bl", "vlen", "alen"):
        local[name].wait()
    got("xaz")
    send("xaf", XA.at[:, zcols], XA.at[:, zcols], nc)
    spread_on("k", KW)
    local["xa"].wait()
    local["wqa"].wait()
    got("xac", "xaf")
    QW[own] = dot(XA[...], WQA[...]).astype(BF)
    spread_x("q", QW)
    spread_y("q", QW)
    send_x(1)
    spread_on("q", QW)
    send_x(2)
    send_x(3)
    v1(0)
    wring1()
    local["x"].wait()
    local["wq"].wait()
    got("xc")
    spread_end("k")
    v2(0)
    spread_end("q")
    a4()
    v1(1)
    wring2()
    v1(2)
    v2(1)
    a5()
    v3(0)
    v2(2)
    v1(3)
    v3(1)
    v2(3)
    a6()
    for name in ("wa0", "wa1"):
        local[name].wait()
        got(name)
    got("ata")
    att = ATTA[...]
    SBA[...] = dot(att, WOAC[:, feat:]).astype(BF)
    send("oza", SBA, RBA, nz)
    OWNA[...] = dot(att, WOAC[:, :feat])
    local["wo"].wait()
    got("woc", "wr2", "wl2")
    v3(2)
    v4(0)
    v3(3)
    for i in range(1, 4):
        v4(i)
    got("oza")
    outa[...] = (OWNA[...] + RBA[...].astype(F32)).astype(BF)
    assert len(sent) == COPIES
    for copy in sent.values():
        copy.wait_send()


def finish(video, audio, outv, outa):
    outv[...] = video[...]
    outa[...] = audio[...]


def per_device(
    video_x, audio_x, video_kv, audio_kv, wq_video, wo_video, wq_audio, wo_audio,
    block_list, video_len, audio_len,
):
    vrows, feat = video_x.shape
    arows = audio_x.shape[0]
    full, width = wq_video.shape
    any_spec = pl.BlockSpec(memory_space=pl.ANY)
    vmem = pl.BlockSpec(memory_space=pltpu.VMEM)

    def V(*shape, dtype=BF):
        return pltpu.VMEM(shape, dtype)

    outs = pl.pallas_call(
        kernel,
        out_shape=[
            jax.ShapeDtypeStruct((vrows, feat), BF),
            jax.ShapeDtypeStruct((arows, feat), BF),
        ],
        in_specs=[any_spec] * 11,
        out_specs=[vmem] * 2,
        scratch_shapes=[
            V(vrows, full), V(arows, full),
            V(vrows, 2, width), V(vrows, 2 * width), V(arows, 2, width),
            V(12, arows, 2 * width), V(12, arows, width),
            V(full, width), V(full, width), V(4 * width, feat), V(2 * width, 2 * feat),
            V(vrows, 4 * width), V(arows, 2 * width),
            V(arows, feat), V(arows, feat), V(arows, feat, dtype=F32),
            V(12 * arows, width + 128), V(12 * arows, width + 128),
            V(2 * arows, width + 128), V(2 * arows, width + 128),
            V(3 * BLOCK, 2 * width),
            pltpu.SMEM(block_list.shape[::-1], jnp.int32), pltpu.SMEM((1,), jnp.int32), pltpu.SMEM((1,), jnp.int32),
            pltpu.SemaphoreType.DMA((12,)),
            pltpu.SemaphoreType.DMA((COPIES,)),
            pltpu.SemaphoreType.DMA((COPIES,)),
        ],
        compiler_params=pltpu.CompilerParams(
            collective_id=0, has_side_effects=True, vmem_limit_bytes=56 * 2**20
        ),
        cost_estimate=pl.CostEstimate(
            flops=4_000_000_000, bytes_accessed=14_000_000, transcendentals=2_000_000
        ),
        name="twin_tower",
    )(
        video_x, audio_x, video_kv, audio_kv, wq_video, wo_video, wq_audio, wo_audio,
        block_list.T, video_len, audio_len,
    )
    return pl.pallas_call(
        finish,
        out_shape=[jax.ShapeDtypeStruct(o.shape, o.dtype) for o in outs],
        in_specs=[vmem] * 2,
        out_specs=[vmem] * 2,
        name="finish",
    )(*outs)


def solution(mesh):
    in_specs = (
        P("vid", "tp"), P("vid", "tp"), P("vid", None, "tp"), P("vid", None, "tp"),
        P(None, "tp"), P("tp", None), P(None, "tp"), P("tp", None), P(), P(), P(),
    )
    return jax.shard_map(
        per_device, mesh=mesh, in_specs=in_specs, out_specs=(P("vid", "tp"), P("vid", "tp")),
        check_vma=False,
    )
```

```python
import math

import jax
import jax.numpy as jnp
from jax import lax
from jax.experimental import pallas as pl
from jax.experimental.pallas import tpu as pltpu
from jax.sharding import PartitionSpec as P

MESH = pl.DeviceIdType.MESH
HDIM = 128
BLOCK = 128
NEG = -1e30
BF = jnp.bfloat16
F32 = jnp.float32
SCALE = HDIM ** (-0.5) * math.log2(math.e)

COPIES = 64


def dot(a, b):
    return jnp.dot(a, b, preferred_element_type=F32)


def dot_t(a, b):
    return lax.dot_general(a, b, (((1,), (1,)), ((), ())), preferred_element_type=F32)


def split3(value):
    hi = value.astype(BF).astype(F32)
    rest = value - hi
    mid = rest.astype(BF).astype(F32)
    return hi, mid, rest - mid


def pack_stats(stats, rows):
    lane = lax.broadcasted_iota(jnp.int32, (rows, 128), 1)
    out = jnp.zeros((rows, 128), F32)
    at = 0
    for value in stats:
        for part in split3(value):
            out = jnp.where(lane == at, part, out)
            at += 1
    return out.astype(BF)


def unpack_stat(tile, at):
    return tile[:, at : at + 1] + tile[:, at + 1 : at + 2] + tile[:, at + 2 : at + 3]


def merge(packed, heads):
    peaks, sums, accs = [], [], []
    for hh in range(heads):
        ms = [unpack_stat(tile, hh * 6) for tile, _ in packed]
        ls = [unpack_stat(tile, hh * 6 + 3) for tile, _ in packed]
        peak = ms[0]
        for m in ms[1:]:
            peak = jnp.maximum(peak, m)
        total, acc = 0.0, 0.0
        for m, l, (_, a) in zip(ms, ls, packed):
            w = jnp.exp2(m - peak)
            total = total + w * l
            acc = acc + w * a[hh]
        peaks.append(peak)
        sums.append(total)
        accs.append(acc)
    return peaks, sums, accs


def kernel(
    x_hbm, xa_hbm, kv_hbm, akv_hbm, wq_hbm, wo_hbm, wqa_hbm, woa_hbm, bl_hbm, vlen_hbm, alen_hbm,
    outv, outa,
    X, XA, kvraw, VK, akraw, KW, QW, WQ, WQA, WOC, WOAC, ATT, ATTA,
    SBA, RBA, OWNA, PS, PR, SX, RX, KS, bl, vlen, alen, lsem, ssem, rsem,
):
    width = WQ.shape[1]
    heads = width // HDIM
    feat = x_hbm.shape[1]
    arows = xa_hbm.shape[0]
    v = lax.axis_index("vid")
    t = lax.axis_index("tp")
    y = lax.rem(v, 4)
    row = lax.div(v, 4)
    h = lax.div(y, 2)
    c = lax.rem(t, 2)
    zl = lax.div(t, 2)
    tz = lax.rem(t + 2, 4)
    tc = t + 1 - 2 * c
    y1, y2, y3 = y + 1 - 2 * lax.rem(y, 2), lax.rem(y + 2, 4), 3 - y
    nz, nc = (v, tz), (v, tc)
    vo = lax.rem(v + 64 + 16 * (2 * zl - 1), 64)
    td = lax.rem(tc + 2, 4)
    no, nd = (vo, tz), (vo, td)
    plane = lax.div(v, 16) * 16
    x = lax.div(v - plane, 4)
    nxr, nxl = (plane + lax.rem(v - plane + 4, 16), t), (plane + lax.rem(v - plane + 12, 16), t)
    ny1, ny2, ny3 = (row * 4 + y1, t), (row * 4 + y2, t), (row * 4 + y3, t)
    nup, ndn = (lax.rem(v + 4, 64), t), (lax.rem(v + 60, 64), t)

    local = {}

    def load(name, i, src, dst):
        local[name] = pltpu.make_async_copy(src, dst, lsem.at[i])
        local[name].start()

    def cols(i, n):
        return pl.ds(pl.multiple_of(i * n, n), n)

    def shard(i):
        return pl.ds(pl.multiple_of(i * arows, arows), arows)

    load("ak", 0, akv_hbm, akraw)
    load("bl", 9, bl_hbm, bl)
    load("vlen", 10, vlen_hbm, vlen)
    load("alen", 11, alen_hbm, alen)
    load("xa", 1, xa_hbm, XA.at[:, cols(t, feat)])
    load("x", 2, x_hbm, X.at[:, cols(t, feat)])
    load("wqa", 3, wqa_hbm, WQA)
    load("wq", 4, wq_hbm, WQ)
    load("kv", 5, kv_hbm, kvraw)
    orow = pl.ds(pl.multiple_of(c * width, width), width)
    load("wo", 6, wo_hbm.at[:, cols(t, feat)], WOC.at[cols(t, width), :])
    load("wa0", 7, woa_hbm.at[:, cols(zl * 2 + c, feat)], WOAC.at[orow, pl.ds(0, feat)])
    load("wa1", 8, woa_hbm.at[:, cols((1 - zl) * 2 + c, feat)], WOAC.at[orow, pl.ds(feat, feat)])

    barrier = pltpu.get_barrier_semaphore()
    for peer in (nz, nc, ny1, ny2, ny3, nup, ndn, no, nd, nxr, nxl):
        pl.semaphore_signal(barrier, inc=1, device_id=peer, device_id_type=MESH)
    own, lower, upper = 4 + y, y, 8 + y
    sel = y + 8 * (1 - h)
    local["ak"].wait()
    KW[own] = akraw[...].reshape(arows, 2 * width)
    pl.semaphore_wait(barrier, 11)

    sent = {}

    def send(name, src, dst, peer):
        i = len(sent)
        sent[name] = pltpu.make_async_remote_copy(
            src_ref=src, dst_ref=dst, send_sem=ssem.at[i], recv_sem=rsem.at[i],
            device_id=peer, device_id_type=MESH,
        )
        sent[name].start()

    def got(*names):
        for name in names:
            sent[name].wait_recv()

    tcols, zcols = cols(t, feat), cols(tz, feat)

    def send_x(i):
        rows = pl.ds(i * BLOCK, BLOCK)
        send(f"xz{i}", x_hbm.at[rows, :], X.at[rows, tcols], nz)

    def spread_x(p, buf):
        send(p + "up", buf.at[own], buf.at[lower], nup)
        send(p + "dn", buf.at[own], buf.at[upper], ndn)

    def spread_y(p, buf):
        send(p + "y1", buf.at[own], buf.at[own], ny1)
        send(p + "y2", buf.at[own], buf.at[own], ny2)
        send(p + "y3", buf.at[own], buf.at[own], ny3)

    def spread_on(p, buf):
        got(p + "up", p + "dn")
        send(p + "f1a", buf.at[lower], buf.at[lower], ny1)
        send(p + "f1b", buf.at[upper], buf.at[upper], ny1)
        send(p + "f2", buf.at[sel], buf.at[sel], ny2)
        send(p + "f3", buf.at[sel], buf.at[sel], ny3)

    def spread_end(p):
        got(*(p + s for s in ("y1", "y2", "y3", "f1a", "f1b", "f2", "f3")))

    send("xaz", xa_hbm, XA.at[:, tcols], nz)
    send("xac", xa_hbm, XA.at[:, tcols], nc)
    spread_x("k", KW)
    send_x(0)
    spread_y("k", KW)
    send("xc", x_hbm, X.at[:, tcols], nc)

    send("woc", wo_hbm.at[:, cols(tc, feat)], WOC.at[cols(t, width), :], nc)
    part4 = width // 4

    def quarter(to, at):
        return pl.ds(pl.multiple_of(to * width + at * part4, part4), part4)

    for name, to, peer in (("woo", tz, no), ("wod", td, nd)):
        send(name, wo_hbm.at[pl.ds(pl.multiple_of(x * part4, part4), part4), cols(to, feat)],
             WOC.at[quarter(t, x), :], peer)

    def wring1():
        got("woo", "wod")
        for tag, to in (("a", tz), ("b", td)):
            rows = quarter(to, x)
            send("wr" + tag, WOC.at[rows, :], WOC.at[rows, :], nxr)
            send("wl" + tag, WOC.at[rows, :], WOC.at[rows, :], nxl)

    def wring2():
        got("wra", "wrb", "wla", "wlb")
        rows = quarter(tz, lax.rem(x + 3, 4))
        send("wr2", WOC.at[rows, :], WOC.at[rows, :], nxr)
        rows = quarter(td, lax.rem(x + 1, 4))
        send("wl2", WOC.at[rows, :], WOC.at[rows, :], nxl)

    send("wa0", woa_hbm.at[:, cols(zl * 2 + 1 - c, feat)], WOAC.at[orow, pl.ds(0, feat)], nc)
    send("wa1", woa_hbm.at[:, cols((1 - zl) * 2 + 1 - c, feat)], WOAC.at[orow, pl.ds(feat, feat)], nc)

    local["kv"].wait()
    VK[...] = kvraw[...].reshape(kvraw.shape[0], 2 * width)

    def v1(i):
        rows = pl.ds(i * BLOCK, BLOCK)
        got(f"xz{i}")
        send(f"xf{i}", X.at[rows, zcols], X.at[rows, zcols], nc)

    lane = lax.broadcasted_iota(jnp.int32, (1, BLOCK), 1)

    def v2(i):
        rows = pl.ds(i * BLOCK, BLOCK)
        vb = v * 4 + i
        entries = [bl[k, vb] for k in range(3)]
        doubles = [None, entries[1] == entries[0],
                   (entries[2] == entries[0]) | (entries[2] == entries[1])]
        bias = []
        for k in range(3):
            slot = jnp.clip(entries[k] - 2 * row + 2, 0, 5)
            for half in range(2):
                KS[pl.ds(k * BLOCK + half * arows, arows), :] = KW[slot * 2 + half]
            limit = alen[0] - entries[k] * BLOCK
            if k:
                limit = jnp.where(doubles[k], 0, limit)
            bias.append(jnp.where(lane < limit, 0.0, NEG))
        bias = jnp.concatenate(bias, axis=1)
        got(f"xf{i}")
        q = dot(X[rows, :], WQ[...]).astype(BF)
        for hh in range(heads):
            hc = pl.ds(hh * HDIM, HDIM)
            s = dot_t(q[:, hh * HDIM : (hh + 1) * HDIM], KS[:, hc]) * SCALE + bias
            e = jnp.exp2(s - jnp.max(s, axis=1, keepdims=True))
            total = jnp.sum(e, axis=1, keepdims=True)
            acc = dot(e.astype(BF), KS[:, pl.ds(width + hh * HDIM, HDIM)])
            ATT[rows, pl.ds(pl.multiple_of(t * width + hh * HDIM, HDIM), HDIM)] = (
                acc / total
            ).astype(BF)
        mine = cols(t, width)
        send(f"az{i}", ATT.at[rows, mine], ATT.at[rows, mine], nz)
        send(f"ac{i}", ATT.at[rows, mine], ATT.at[rows, mine], nc)

    def v3(i):
        rows = pl.ds(i * BLOCK, BLOCK)
        other = cols(tz, width)
        got(f"az{i}")
        send(f"af{i}", ATT.at[rows, other], ATT.at[rows, other], nc)

    def v4(i):
        rows = pl.ds(i * BLOCK, BLOCK)
        got(f"ac{i}", f"af{i}")
        outv[rows, :] = dot(ATT[rows, :], WOC[...]).astype(BF)

    def a4():
        base = v * 4

        def block(j):
            g = h + j
            blk = 2 * row - 2 + g
            bias = []
            for k in range(4):
                vb = base + k
                linked = (bl[0, vb] == blk) | (bl[1, vb] == blk) | (bl[2, vb] == blk)
                limit = jnp.where(linked, vlen[0] - vb * BLOCK, 0)
                bias.append(jnp.where(lane < limit, 0.0, NEG))
            bias = jnp.concatenate(bias, axis=1)
            rows = pl.ds(pl.multiple_of(g * BLOCK, BLOCK), BLOCK)
            stats = []
            qs = jnp.concatenate([QW[2 * g], QW[2 * g + 1]], axis=0)
            for hh in range(heads):
                hc = pl.ds(hh * HDIM, HDIM)
                s = dot_t(qs[:, hh * HDIM : (hh + 1) * HDIM], VK[:, hc]) * SCALE + bias
                m = jnp.max(s, axis=1, keepdims=True)
                e = jnp.exp2(s - m)
                stats += [m, jnp.sum(e, axis=1, keepdims=True)]
                PS[rows, hc] = dot(e.astype(BF), VK[:, pl.ds(width + hh * HDIM, HDIM)]).astype(BF)
            PS[rows, pl.ds(width, 128)] = pack_stats(stats, BLOCK)

        def give(name, index, slot, peer):
            send(name, PS.at[shard(index), :], PR.at[pl.ds(slot * arows, arows), :], peer)

        for j in (1, 3):
            block(j)
        give("p2a", 4 + y2, 6, ny2)
        give("p3a", 4 + y3, 9, ny3)
        give("p2b", y2 + 8 * h, 7, ny2)
        give("p3b", y3 + 8 * h, 10, ny3)
        block(0)
        give("p1a", y1, 3, ny1)
        block(4)
        give("p1c", 8 + y1, 5, ny1)
        block(2)
        give("p1b", 4 + y1, 4, ny1)

    def part(buf, index):
        rows = shard(index)
        return (
            buf[rows, pl.ds(width, 128)].astype(F32),
            [buf[rows, pl.ds(hh * HDIM, HDIM)].astype(F32) for hh in range(heads)],
        )

    def put(index, state):
        rows = shard(index)
        peaks, sums, accs = state
        stats = []
        for hh in range(heads):
            SX[rows, pl.ds(hh * HDIM, HDIM)] = accs[hh].astype(BF)
            stats += [peaks[hh], sums[hh]]
        SX[rows, pl.ds(width, 128)] = pack_stats(stats, arows)

    def a5():
        got("p1a", "p1b", "p1c", "p2a", "p2b", "p3a", "p3b")
        put(1 - h, merge([part(PS, y + 8 * (1 - h)), part(PR, 3 + 2 * (1 - h)),
                          part(PR, 7), part(PR, 10)], heads))
        put(h, merge([part(PS, y + 8 * h), part(PR, 3 + 2 * h)], heads))
        send("pup", SX.at[pl.ds(arows, arows), :], RX.at[pl.ds(0, arows), :], nup)
        send("pdn", SX.at[pl.ds(0, arows), :], RX.at[pl.ds(arows, arows), :], ndn)

    def a6():
        got("pup", "pdn")
        _, sums, accs = merge(
            [part(PS, 4 + y), part(PR, 4), part(PR, 6), part(PR, 9), part(RX, 0), part(RX, 1)], heads
        )
        for hh in range(heads):
            ATTA[:, pl.ds(pl.multiple_of(c * width + hh * HDIM, HDIM), HDIM)] = (
                accs[hh] / sums[hh]
            ).astype(BF)
        mine = cols(c, width)
        send("ata", ATTA.at[:, mine], ATTA.at[:, mine], nc)

    for name in ("bl", "vlen", "alen"):
        local[name].wait()
    got("xaz")
    send("xaf", XA.at[:, zcols], XA.at[:, zcols], nc)
    spread_on("k", KW)
    local["xa"].wait()
    local["wqa"].wait()
    got("xac", "xaf")
    QW[own] = dot(XA[...], WQA[...]).astype(BF)
    spread_x("q", QW)
    spread_y("q", QW)
    send_x(1)
    spread_on("q", QW)
    send_x(2)
    send_x(3)
    v1(0)
    wring1()
    local["x"].wait()
    local["wq"].wait()
    got("xc")
    spread_end("k")
    v2(0)
    spread_end("q")
    a4()
    v1(1)
    wring2()
    v1(2)
    v2(1)
    a5()
    v3(0)
    v2(2)
    v1(3)
    v3(1)
    v2(3)
    a6()
    for name in ("wa0", "wa1"):
        local[name].wait()
        got(name)
    v3(2)
    got("ata")
    att = ATTA[...]
    SBA[...] = dot(att, WOAC[:, feat:]).astype(BF)
    send("oza", SBA, RBA, nz)
    OWNA[...] = dot(att, WOAC[:, :feat])
    local["wo"].wait()
    got("woc", "wr2", "wl2")
    v4(0)
    v3(3)
    for i in range(1, 4):
        v4(i)
    got("oza")
    outa[...] = (OWNA[...] + RBA[...].astype(F32)).astype(BF)
    assert len(sent) == COPIES
    for copy in sent.values():
        copy.wait_send()


def finish(video, audio, outv, outa, bufv, bufa, sem_in, sem_out):
    rows = video.shape[0] // 4
    parts = [(video, bufv, outv, pl.ds(i * rows, rows)) for i in range(4)]
    parts.append((audio, bufa, outa, pl.ds(0, audio.shape[0])))
    copies = [
        (
            pltpu.make_async_copy(src.at[at], buf.at[at], sem_in.at[i]),
            pltpu.make_async_copy(buf.at[at], dst.at[at], sem_out.at[i]),
        )
        for i, (src, buf, dst, at) in enumerate(parts)
    ]
    for first, _ in copies:
        first.start()
    for first, second in copies:
        first.wait()
        second.start()
    for _, second in copies:
        second.wait()


def per_device(
    video_x, audio_x, video_kv, audio_kv, wq_video, wo_video, wq_audio, wo_audio,
    block_list, video_len, audio_len,
):
    vrows, feat = video_x.shape
    arows = audio_x.shape[0]
    full, width = wq_video.shape
    any_spec = pl.BlockSpec(memory_space=pl.ANY)
    vmem = pl.BlockSpec(memory_space=pltpu.VMEM)

    def V(*shape, dtype=BF):
        return pltpu.VMEM(shape, dtype)

    outs = pl.pallas_call(
        kernel,
        out_shape=[
            jax.ShapeDtypeStruct((vrows, feat), BF),
            jax.ShapeDtypeStruct((arows, feat), BF),
        ],
        in_specs=[any_spec] * 11,
        out_specs=[vmem] * 2,
        scratch_shapes=[
            V(vrows, full), V(arows, full),
            V(vrows, 2, width), V(vrows, 2 * width), V(arows, 2, width),
            V(12, arows, 2 * width), V(12, arows, width),
            V(full, width), V(full, width), V(4 * width, feat), V(2 * width, 2 * feat),
            V(vrows, 4 * width), V(arows, 2 * width),
            V(arows, feat), V(arows, feat), V(arows, feat, dtype=F32),
            V(12 * arows, width + 128), V(12 * arows, width + 128),
            V(2 * arows, width + 128), V(2 * arows, width + 128),
            V(3 * BLOCK, 2 * width),
            pltpu.SMEM(block_list.shape[::-1], jnp.int32), pltpu.SMEM((1,), jnp.int32), pltpu.SMEM((1,), jnp.int32),
            pltpu.SemaphoreType.DMA((12,)),
            pltpu.SemaphoreType.DMA((COPIES,)),
            pltpu.SemaphoreType.DMA((COPIES,)),
        ],
        compiler_params=pltpu.CompilerParams(
            collective_id=0, has_side_effects=True, vmem_limit_bytes=56 * 2**20
        ),
        cost_estimate=pl.CostEstimate(
            flops=4_000_000_000, bytes_accessed=14_000_000, transcendentals=2_000_000
        ),
        name="twin_tower",
    )(
        video_x, audio_x, video_kv, audio_kv, wq_video, wo_video, wq_audio, wo_audio,
        block_list.T, video_len, audio_len,
    )
    return pl.pallas_call(
        finish,
        out_shape=[jax.ShapeDtypeStruct(o.shape, o.dtype) for o in outs],
        in_specs=[any_spec] * 2,
        out_specs=[any_spec] * 2,
        scratch_shapes=[
            V(vrows, feat), V(arows, feat),
            pltpu.SemaphoreType.DMA((5,)), pltpu.SemaphoreType.DMA((5,)),
        ],
        name="finish",
    )(*outs)


def solution(mesh):
    in_specs = (
        P("vid", "tp"), P("vid", "tp"), P("vid", None, "tp"), P("vid", None, "tp"),
        P(None, "tp"), P("tp", None), P(None, "tp"), P("tp", None), P(), P(), P(),
    )
    return jax.shard_map(
        per_device, mesh=mesh, in_specs=in_specs, out_specs=(P("vid", "tp"), P("vid", "tp")),
        check_vma=False,
    )
```
